32 devices in a mesh: tile: 8 (over z, y), day: 4 (over x, core).
Axes of the slice: x: 2, y: 2, z: 4, core: 2. Of those that a mesh axis runs over, the one named last changes fastest.
Arguments:
- coarse: bfloat16 [8, 20, 128, 256], P('day', None, 'tile'), may hold values from -6 to 6
- fine: bfloat16 [8, 4, 2048, 4096], P('day', None, 'tile'), may hold values from -6 to 6
- coarse_lat: bfloat16 [128, 64], P('tile'), may hold values from -0.5 to 0.5
- coarse_lon: bfloat16 [256, 64], replicated, may hold values from -0.375 to 0.375
- coarse_var: bfloat16 [20, 8], replicated, may hold values from -1.25 to 1.25
- fine_lat: bfloat16 [2048, 64], P('tile'), may hold values from -0.75 to 0.75
- fine_lon: bfloat16 [4096, 64], replicated, may hold values from -0.75 to 0.75
- fine_var: bfloat16 [4, 8], replicated, may hold values from -2 to 2
Outputs:
- grad_fine_lat: float32 [2048, 64], P('tile')
- grad_fine_lon: float32 [4096, 64], P('tile')
- grad_fine_var: float32 [4, 8], replicated
- grad_coarse_lat: float32 [128, 64], P('tile')
- grad_coarse_lon: float32 [256, 64], replicated
- grad_coarse_var: float32 [20, 8], replicated
The draws below stay inside these ranges and needn't reach their ends.
All inputs are finite; a program needn't handle non-finite values.
Results may differ from the reference program's by a relative error of at most 0.00065.
Values sent between devices are 32-bit elements; how exact they have to be, the bound alone decides.
A program may use at most 128 MiB of HBM per device.

```python
import math
import jax
import jax.numpy as jnp
from jax import lax

D1 = 128
D2 = 256
D3 = 20
R1 = 64
R2 = 64
R3 = 8
F1 = 2048
F2 = 4096
F3 = 4
DAYS = 8


def strengthened(entries, own_key, source, target, parts, factor):
    owner, partner = [(jnp.arange(entries.shape[dim]) // (entries.shape[dim] // parts)).reshape([-1 if axis == dim else 1 for axis in range(entries.ndim)]) for dim in (source, target)]
    chosen = jax.random.permutation(own_key, parts)[partner]
    strong = (owner == chosen) | (owner == (partner + parts // 2) % parts)
    return jnp.where(strong, factor * entries, entries)


def level_of(key, shape, pieces, smallest, high):
    factor_of, own = 1.0, jax.random.fold_in(key, 6)
    for axis_at, parts in pieces:
        steps = jnp.exp(jax.random.uniform(jax.random.fold_in(own, axis_at), (parts,), jnp.float32, smallest / len(pieces), high / len(pieces)))
        factor_of = factor_of * jnp.repeat(steps, shape[axis_at] // parts).reshape([-1 if axis == axis_at else 1 for axis in range(len(shape))])
    return factor_of


def noise(stream_key, extent, scale, limit, cuts=(), kind=jnp.bfloat16):
    gain = level_of(stream_key, extent, cuts, -0.22, 0.18) if cuts else 1.0
    values = jax.random.normal(stream_key, extent, jnp.float32) * scale * gain
    return jnp.minimum(jnp.maximum(values, -limit), limit).astype(kind)


def bell_draw_with(key, extent, scale, limit, shards, heavy, held_as=jnp.bfloat16):
    values = scale * jax.random.normal(key, extent, jnp.float32)
    if shards:
        values = values * level_of(key, extent, shards, -0.22, 0.18)
    return jnp.clip(strengthened(values, jax.random.fold_in(key, 3), *heavy), -limit, limit).astype(held_as)


def setup_inputs(seed: int = 0) -> dict:
    key_of = jax.random.split(jax.random.key(seed), 9)
    return {
        "coarse": noise(key_of[0], (DAYS, D3, D1, D2), 1.0, 6.0, ((0, 4), (2, 8))),
        "fine": bell_draw_with(key_of[1], (DAYS, F3, F1, F2), 1.0, 6.0, ((0, 4), (2, 8)), (2, 3, 8, 2.0)),
        "coarse_lat": noise(key_of[2], (D1, R1), D1 ** -0.5, 0.5, ((0, 8),)),
        "coarse_lon": noise(key_of[3], (D2, R2), D2 ** -0.5, 0.375),
        "coarse_var": noise(key_of[4], (D3, R3), D3 ** -0.5, 1.25),
        "fine_lat": noise(key_of[5], (F1, R1), R1 ** -0.5, 0.75, ((0, 8),)),
        "fine_lon": noise(key_of[6], (F2, R2), R2 ** -0.5, 0.75),
        "fine_var": noise(key_of[7], (F3, R3), R3 ** -0.5, 2.0),
    }


HIGHEST = lax.Precision.HIGHEST

def rows_by_factor(matrix, factor):
    return lax.dot_general(matrix, factor, (((1,), (1,)), ((), ())), preferred_element_type=jnp.float32)

def outer_rows(left, right):
    return lax.dot_general(left, right, (((0,), (0,)), ((), ())), preferred_element_type=jnp.float32)

def project(coarse, lat_float, coarse_lon, var_float):
    days, chans, lats, lons = coarse.shape
    along = jnp.dot(coarse.reshape(-1, lons), coarse_lon, preferred_element_type=jnp.float32)
    along = along.reshape(days, chans, lats, coarse_lon.shape[1])
    core = jnp.einsum('ncar,as,ct->nsrt', along, lat_float, var_float, precision=HIGHEST)
    return (along, core)

def day_terms(core, fine, fine_lat_float, fine_lon, fine_var_float):

    def advance(carry, inputs):
        grad_first, grad_second, grad_third = carry
        day_core, day_fine = inputs
        mixed = jnp.einsum('is,srt->irt', fine_lat_float, day_core, precision=HIGHEST)
        lifted = jnp.einsum('irt,vt->vir', mixed, fine_var_float, precision=HIGHEST).astype(jnp.bfloat16)
        flat_lifted = lifted.reshape(-1, lifted.shape[2])
        predicted = rows_by_factor(flat_lifted, fine_lon)
        target = day_fine.reshape(predicted.shape).astype(jnp.float32)
        residual = (predicted - target).astype(jnp.bfloat16)
        back = jnp.dot(residual, fine_lon, preferred_element_type=jnp.float32).reshape(lifted.shape)
        grad_second = grad_second + outer_rows(residual, flat_lifted)
        grad_first = grad_first + jnp.einsum('vir,srt,vt->is', back, day_core, fine_var_float, precision=HIGHEST)
        grad_third = grad_third + jnp.einsum('vir,irt->vt', back, mixed, precision=HIGHEST)
        day_grad = jnp.einsum('vir,is,vt->srt', back, fine_lat_float, fine_var_float, precision=HIGHEST)
        return ((grad_first, grad_second, grad_third), day_grad)
    start = (jnp.zeros(fine_lat_float.shape, jnp.float32), jnp.zeros(fine_lon.shape, jnp.float32), jnp.zeros(fine_var_float.shape, jnp.float32))
    return lax.scan(advance, start, (core, fine))

def coarse_grads(coarse, coarse_lat, along, lat_float, var_float, core_grad):
    days, chans, lats, lons = coarse.shape
    first = jnp.einsum('ncar,ct,nsrt->as', along, var_float, core_grad, precision=HIGHEST)
    flipped = jnp.transpose(coarse, (0, 1, 3, 2)).reshape(-1, lats)
    lat_coarse = jnp.dot(flipped, coarse_lat, preferred_element_type=jnp.float32)
    lat_coarse = lat_coarse.reshape(days, chans, lons, coarse_lat.shape[1])
    weighted = jnp.einsum('ct,nsrt->ncsr', var_float, core_grad, precision=HIGHEST)
    second = jnp.einsum('ncbs,ncsr->br', lat_coarse, weighted, precision=HIGHEST)
    third = jnp.einsum('ncar,as,nsrt->ct', along, lat_float, core_grad, precision=HIGHEST)
    return (first, second, third)

def reference(coarse, fine, coarse_lat, coarse_lon, coarse_var, fine_lat, fine_lon, fine_var):
    lat_float = coarse_lat.astype(jnp.float32)
    var_float = coarse_var.astype(jnp.float32)
    fine_lat_float = fine_lat.astype(jnp.float32)
    fine_var_float = fine_var.astype(jnp.float32)
    along, core = project(coarse, lat_float, coarse_lon, var_float)
    totals, day_grads = day_terms(core, fine, fine_lat_float, fine_lon, fine_var_float)
    core_grad = day_grads * math.sqrt(R1 * R2 * R3 / (F1 * F2 * F3))
    first, second, third = coarse_grads(coarse, coarse_lat, along, lat_float, var_float, core_grad)
    days = coarse.shape[0]
    return (totals[0] / math.sqrt(days * F3 * F2), totals[1] / math.sqrt(days * F3 * F1), totals[2] / math.sqrt(days * F1 * F2), first / math.sqrt(days * R2 * R3), second / math.sqrt(days * R1 * R3), third / math.sqrt(days * R1 * R2))
```

```python
import functools
import math

import jax
import jax.numpy as jnp
from jax import lax
from jax.experimental import pallas as pl
from jax.experimental.pallas import tpu as pltpu
from jax.sharding import PartitionSpec as P

F32 = jnp.float32
BF16 = jnp.bfloat16
MESH = pl.DeviceIdType.MESH
LANES = 128


def dot(left, right):
    return jnp.dot(left, right, preferred_element_type=F32)


def dot_nt(left, right):
    return lax.dot_general(left, right, (((1,), (1,)), ((), ())), preferred_element_type=F32)


def halves(value):
    high = value.astype(BF16)
    return high, (value - high.astype(F32)).astype(BF16)


def dot_exact(left, right):
    high, low = halves(right)
    return dot(left, high) + dot(left, low)


def dot_nt_three(left, right):
    lh, ll = halves(left)
    rh, rl = halves(right)
    return dot_nt(lh, rh) + (dot_nt(lh, rl) + dot_nt(ll, rh))


def kernel(
    d,
    cvar, fvar, coarse, clat, clon, flat, flon, fine,
    o_flat, o_flon, o_fin, o_small, o_clat,
    fbuf, along, wall, wfl, core, mixed, lifted, lifted_t, lon_pad, lon_pad_t,
    back, spread, fva, gl, gday, gown, gtile, gfin,
    qsend, qrecv, vv, xs, lat_day, clat_day, fsend, frecv, fday, fall,
    s_fine, s_w, r_w, s_q, r_q, s_gd, r_gd, s_gt, r_gt, s_gf, r_gf,
    s_ld, r_ld, s_cd, r_cd, s_fs, r_fs, s_fd, r_fd, s_fa, r_fa,
):
    T, DAY, N, C, A, R, S, TR, V, I, J = (
        d["T"], d["DAY"], d["N"], d["C"], d["A"], d["R"], d["S"], d["TR"], d["V"], d["I"], d["J"]
    )
    JB, NB, NSUB, jb, rq, rr = d["JB"], d["NB"], d["NSUB"], d["jb"], d["rq"], d["rr"]
    L = N * R
    me = lax.axis_index("tile")
    day = lax.axis_index("day")
    first = lax.rem(lax.div(me * jb, JB) + 1, NB)

    def block_of(k):
        return lax.rem(first + k, NB)

    def fine_copy(k):
        columns = pl.ds(pl.multiple_of(block_of(k) * JB, JB), JB)
        return pltpu.make_async_copy(fine.at[:, :, :, columns], fbuf.at[k], s_fine.at[k])

    @pl.loop(0, NB)
    def _(k):
        fine_copy(k).start()

    barrier = pltpu.get_barrier_semaphore()

    @pl.loop(1, T)
    def _(off):
        pl.semaphore_signal(barrier, inc=1, device_id={"tile": lax.rem(me + off, T)}, device_id_type=MESH)

    @pl.loop(1, DAY)
    def _(off):
        pl.semaphore_signal(barrier, inc=1, device_id={"day": lax.rem(day + off, DAY)}, device_id_type=MESH)

    def tile_copy(src, dst, ssem, rsem, peer):
        return pltpu.make_async_remote_copy(
            src_ref=src, dst_ref=dst, send_sem=ssem, recv_sem=rsem,
            device_id={"tile": peer}, device_id_type=MESH,
        )

    def day_copy(src, dst, ssem, rsem, peer):
        return pltpu.make_async_remote_copy(
            src_ref=src, dst_ref=dst, send_sem=ssem, recv_sem=rsem,
            device_id={"day": peer}, device_id_type=MESH,
        )

    row = lax.broadcasted_iota(jnp.int32, (R, L), 0)
    column = lax.broadcasted_iota(jnp.int32, (R, L), 1)
    total = None
    for n in range(N):
        place = jnp.where(row + n * R == column, 1.0, 0.0).astype(BF16)
        factor = dot(clon[...], place).astype(BF16)
        part = dot(coarse[n], factor)
        total = part if total is None else total + part
    along[...] = total.reshape(C, A, L)
    for t in range(TR):
        acc = cvar[0, t] * along[0]
        for c in range(1, C):
            acc = acc + cvar[c, t] * along[c]
        wall[me, t] = acc
    wall[me, TR] = jnp.zeros((A, L), F32)
    wall[me, TR, :, 0:S] = clat[...].astype(F32)

    pl.semaphore_wait(barrier, T - 1 + DAY - 1)

    def w_copy(slot, off, peer):
        return tile_copy(wall.at[slot], wall.at[slot], s_w.at[off], r_w.at[off], peer)

    @pl.loop(1, T)
    def _(off):
        w_copy(me, off, lax.rem(me + off, T)).start()

    for n in range(N):
        place = jnp.where(row + n * R == column, 1.0, 0.0).astype(BF16)
        place_t = jnp.where(
            lax.broadcasted_iota(jnp.int32, (L, R), 1) + n * R
            == lax.broadcasted_iota(jnp.int32, (L, R), 0), 1.0, 0.0
        ).astype(BF16)

        @pl.loop(0, NB)
        def _(b):
            rows = pl.ds(pl.multiple_of(b * JB, JB), JB)
            block = flon[rows, :]
            lon_pad[n, rows, :] = dot(block, place).astype(BF16)
            lon_pad_t[n, b] = dot_nt(place_t, block).astype(BF16)

    back[...] = jnp.zeros_like(back)
    fva[...] = jnp.zeros_like(fva)
    xs[...] = jnp.zeros_like(xs)
    qsend[:, TR] = jnp.zeros((T, A, L), F32)
    if rr < 8:
        fsend[...] = jnp.zeros_like(fsend)

    @pl.loop(1, T)
    def _(off):
        w_copy(lax.rem(me - off + T, T), off, lax.rem(me + off, T)).wait_recv()

    for t in range(TR):
        wfl[:, t * L:(t + 1) * L] = wall[:, t].reshape(T * A, L)
    lat_all = wall[:, TR].reshape(T * A, L)
    lat_t = jnp.transpose(lat_all)[0:S].astype(BF16)
    core[...] = dot_exact(lat_t, wfl[...])
    mixed[...] = dot_exact(flat[...], core[...])

    CH = min(32, I)

    @pl.loop(0, I // CH)
    def _(q):
        rows = pl.ds(pl.multiple_of(q * CH, CH), CH)
        for v in range(V):
            acc = fvar[v, 0] * mixed[rows, 0:L]
            for t in range(1, TR):
                acc = acc + fvar[v, t] * mixed[rows, t * L:(t + 1) * L]
            lifted[v, rows, :] = acc.astype(BF16)

    for v in range(V):
        lifted_t[v] = jnp.transpose(lifted[v].astype(F32)).astype(BF16)

    def gd_send(k, off):
        to = lax.rem(day + off, DAY)
        return day_copy(
            gl.at[k, :, pl.ds(pl.multiple_of(to * rq, rq), rq), :], gday.at[k, day],
            s_gd.at[k, off], r_gd.at[k, off], to,
        )

    def gd_recv(k, off):
        source = lax.rem(day - off + DAY, DAY)
        return day_copy(
            gl.at[k, :, pl.ds(pl.multiple_of(day * rq, rq), rq), :], gday.at[k, source],
            s_gd.at[k, off], r_gd.at[k, off], source,
        )

    def gt_send(k, q, owner):
        off = lax.rem(owner - me + T, T)
        return tile_copy(gown.at[k, q], gtile.at[me], s_gt.at[off], r_gt.at[off], owner)

    def gt_recv(off):
        source = lax.rem(me - off + T, T)
        return tile_copy(gown.at[0, 0], gtile.at[source], s_gt.at[off], r_gt.at[off], source)

    def pass_on(k):
        for off in range(1, DAY):
            gd_recv(k, off).wait_recv()
        acc = gday[k, 0]
        for e in range(1, DAY):
            acc = acc + gday[k, e]
        gown[k] = acc
        for q in range(NSUB):
            owner = block_of(k) * NSUB + q

            @pl.when(owner != me)
            def _():
                gt_send(k, q, owner).start()

            @pl.when(owner == me)
            def _():
                gtile[me] = acc[q]

    @pl.loop(0, NB)
    def _(k):
        fine_copy(k).wait()
        b = block_of(k)
        rows = pl.ds(pl.multiple_of(b * JB, JB), JB)
        grad = None
        for v in range(V):
            term = None
            for n in range(N):
                predicted = dot(lifted[v], lon_pad_t[n, b])
                residual = (predicted - fbuf[k, n, v].astype(F32)).astype(BF16)
                part = dot(residual, lon_pad[n, rows, :])
                term = part if term is None else term + part
                piece = dot(lifted_t[v, n * R:(n + 1) * R, :], residual)
                grad = piece if grad is None else grad + piece
            back[v] += term
        for q in range(NSUB):
            gl[k, q] = grad[:, q * jb:(q + 1) * jb]
        gday[k, day] = gl[k, :, pl.ds(pl.multiple_of(day * rq, rq), rq), :]
        for off in range(1, DAY):
            gd_send(k, off).start()

        @pl.when(k >= 2)
        def _():
            pass_on(k - 2)

    @pl.loop(0, I // CH)
    def _(q):
        rows = pl.ds(pl.multiple_of(q * CH, CH), CH)
        for t in range(TR):
            acc = fvar[0, t] * back[0, rows, :]
            for v in range(1, V):
                acc = acc + fvar[v, t] * back[v, rows, :]
            spread[rows, t * L:(t + 1) * L] = acc

    scale = math.sqrt(S * R * TR / (I * T * J * V))
    flat_t = jnp.transpose(flat[...].astype(F32)).astype(BF16)
    core_grad = dot_exact(flat_t, spread[...]) * scale
    wanted = dot_exact(lat_all[:, 0:S].astype(BF16), core_grad)
    for t in range(TR):
        qsend[:, t] = wanted[:, t * L:(t + 1) * L].reshape(T, A, L)
    qsend[:, TR, :, 0:S] = dot_nt_three(wfl[...], core_grad).reshape(T, A, S)
    qrecv[me] = qsend[me]

    def q_send(off):
        peer = lax.rem(me + off, T)
        return tile_copy(qsend.at[peer], qrecv.at[me], s_q.at[off], r_q.at[off], peer)

    def q_recv(off):
        source = lax.rem(me - off + T, T)
        return tile_copy(qsend.at[me], qrecv.at[source], s_q.at[off], r_q.at[off], source)

    @pl.loop(1, T)
    def _(off):
        q_send(off).start()

    for k in range(max(NB - 2, 0), NB):
        pass_on(k)

    lat_day[day] = dot_nt_three(spread[...], core[...])

    def own_send(buf, ssem, rsem, off):
        return day_copy(buf.at[day], buf.at[day], ssem.at[off], rsem.at[off], lax.rem(day + off, DAY))

    def own_recv(buf, ssem, rsem, off):
        source = lax.rem(day - off + DAY, DAY)
        return day_copy(buf.at[source], buf.at[source], ssem.at[off], rsem.at[off], source)

    for off in range(1, DAY):
        own_send(lat_day, s_ld, r_ld, off).start()

    @pl.loop(0, I // CH)
    def _(q):
        rows = pl.ds(pl.multiple_of(q * CH, CH), CH)
        for v in range(V):
            held = back[v, rows, :]
            for t in range(TR):
                product = held * mixed[rows, t * L:(t + 1) * L]
                fva[v * TR + t] += jnp.sum(product.reshape(CH // 8, 8, L), axis=0)

    xs[C * TR:C * TR + V * TR, :] = jnp.sum(fva[...], axis=1)

    @pl.loop(1, T)
    def _(off):
        q_recv(off).wait_recv()

    summed = qrecv[0]
    for p in range(1, T):
        summed = summed + qrecv[p]
    clat_day[day] = summed[TR]
    for off in range(1, DAY):
        own_send(clat_day, s_cd, r_cd, off).start()
    q_of = summed[0:TR]
    for c in range(C):
        acc = cvar[c, 0] * q_of[0]
        for t in range(1, TR):
            acc = acc + cvar[c, t] * q_of[t]
        vv[c * A:(c + 1) * A, :] = acc
        xs[c * TR:(c + 1) * TR, :] = jnp.sum(along[c][None] * q_of, axis=1)
    v_high, v_low = halves(jnp.transpose(vv[...]))
    lon_t = None
    for n in range(N):
        mine = slice(n * R, (n + 1) * R)
        part = dot(v_high[mine], coarse[n]) + dot(v_low[mine], coarse[n])
        lon_t = part if lon_t is None else lon_t + part
    x_high, x_low = halves(xs[...])
    ones = jnp.ones((8, L), BF16)
    small = dot_nt(ones, x_high) + dot_nt(ones, x_low)
    B = lon_t.shape[1]
    for p in range(T):
        fsend[p, 0, 0:rr, :] = lon_t[p * rr:(p + 1) * rr, :]
        fsend[p, 1] = small
    frecv[me] = fsend[me]

    def f_send(off):
        peer = lax.rem(me + off, T)
        return tile_copy(fsend.at[peer], frecv.at[me], s_fs.at[off], r_fs.at[off], peer)

    def f_recv(off):
        source = lax.rem(me - off + T, T)
        return tile_copy(fsend.at[me], frecv.at[source], s_fs.at[off], r_fs.at[off], source)

    @pl.loop(1, T)
    def _(off):
        f_send(off).start()

    @pl.loop(1, T)
    def _(off):
        gt_recv(off).wait_recv()

    rows_sum = gtile[0]
    for p in range(1, T):
        rows_sum = rows_sum + gtile[p]
    gfin[day] = rows_sum
    for off in range(1, DAY):
        own_send(gfin, s_gf, r_gf, off).start()

    @pl.loop(1, T)
    def _(off):
        f_recv(off).wait_recv()

    fsum = frecv[0]
    for p in range(1, T):
        fsum = fsum + frecv[p]
    fday[day] = fsum
    for off in range(1, DAY):
        own_send(fday, s_fd, r_fd, off).start()

    days = N * DAY
    for off in range(1, DAY):
        own_recv(lat_day, s_ld, r_ld, off).wait_recv()
    acc = lat_day[0]
    for e in range(1, DAY):
        acc = acc + lat_day[e]
    o_flat[...] = acc * (1.0 / math.sqrt(days * V * J))
    for off in range(1, DAY):
        own_recv(clat_day, s_cd, r_cd, off).wait_recv()
    acc = clat_day[0]
    for e in range(1, DAY):
        acc = acc + clat_day[e]
    o_clat[...] = acc * (1.0 / math.sqrt(days * R * TR))

    for off in range(1, DAY):
        own_recv(fday, s_fd, r_fd, off).wait_recv()
    ftotal = fday[0]
    for e in range(1, DAY):
        ftotal = ftotal + fday[e]
    fall[me] = ftotal[0]

    def a_copy(slot, off, peer):
        return tile_copy(fall.at[slot], fall.at[slot], s_fa.at[off], r_fa.at[off], peer)

    @pl.loop(1, T)
    def _(off):
        a_copy(me, off, lax.rem(me + off, T)).start()

    o_small[...] = ftotal[1]
    for off in range(1, DAY):
        own_recv(gfin, s_gf, r_gf, off).wait_recv()
    o_flon[...] = gfin[...] * (1.0 / math.sqrt(days * V * I * T))

    @pl.loop(1, T)
    def _(off):
        a_copy(lax.rem(me - off + T, T), off, lax.rem(me + off, T)).wait_recv()

    o_fin[...] = fall[...] * (1.0 / math.sqrt(days * S * TR))

    @pl.loop(1, T)
    def _(off):
        w_copy(me, off, lax.rem(me + off, T)).wait_send()
        q_send(off).wait_send()
        gt_recv(off).wait_send()
        f_send(off).wait_send()
        a_copy(me, off, lax.rem(me + off, T)).wait_send()

    for off in range(1, DAY):
        own_send(lat_day, s_ld, r_ld, off).wait_send()
        own_send(clat_day, s_cd, r_cd, off).wait_send()
        own_send(gfin, s_gf, r_gf, off).wait_send()
        own_send(fday, s_fd, r_fd, off).wait_send()

        @pl.loop(0, NB)
        def _(k):
            gd_send(k, off).wait_send()


def per_device(T, DAY, coarse, fine, coarse_lat, coarse_lon, coarse_var, fine_lat, fine_lon, fine_var):
    N, C, a_own, B = coarse.shape
    A = -(-a_own // 8) * 8
    if A != a_own:
        coarse = jnp.pad(coarse, ((0, 0), (0, 0), (0, A - a_own), (0, 0)))
        coarse_lat = jnp.pad(coarse_lat, ((0, A - a_own), (0, 0)))
    R, S, TR = coarse_lon.shape[1], coarse_lat.shape[1], coarse_var.shape[1]
    V, I, J = fine.shape[1], fine.shape[2], fine.shape[3]
    jb = J // T
    JB = max(512, jb)
    NB, NSUB = J // JB, JB // jb
    rq, rr = R // DAY, R // T
    RP = max(rr, 8)
    L = N * R
    W = TR * L
    XS = -(-(C * TR + V * TR) // LANES) * LANES
    XS = max(XS, B)
    d = dict(T=T, DAY=DAY, N=N, C=C, A=A, R=R, S=S, TR=TR, V=V, I=I, J=J,
             JB=JB, NB=NB, NSUB=NSUB, jb=jb, rq=rq, rr=rr)
    vmem = pl.BlockSpec(memory_space=pltpu.VMEM)
    smem = pl.BlockSpec(memory_space=pltpu.SMEM)
    dma = lambda *shape: pltpu.SemaphoreType.DMA(shape)
    buf = lambda *shape: pltpu.VMEM(shape, F32)
    half = lambda *shape: pltpu.VMEM(shape, BF16)
    o_flat, o_flon, o_fin, o_small, o_clat = pl.pallas_call(
        functools.partial(kernel, d),
        out_shape=(
            jax.ShapeDtypeStruct((I, S), F32),
            jax.ShapeDtypeStruct((DAY, rq, jb), F32),
            jax.ShapeDtypeStruct((T, RP, B), F32),
            jax.ShapeDtypeStruct((8, XS), F32),
            jax.ShapeDtypeStruct((A, L), F32),
        ),
        in_specs=[smem, smem, vmem, vmem, vmem, vmem, vmem, pl.BlockSpec(memory_space=pl.ANY)],
        out_specs=(vmem,) * 5,
        scratch_shapes=[
            half(NB, N, V, I, JB), buf(C, A, L), buf(T, TR + 1, A, L), buf(T * A, W), buf(S, W),
            buf(I, W), half(V, I, L), half(V, L, I), half(N, J, L), half(N, NB, L, JB),
            buf(V, I, L), buf(I, W), buf(V * TR, 8, L), buf(NB, NSUB, R, jb),
            buf(NB, DAY, NSUB, rq, jb), buf(NB, NSUB, rq, jb), buf(T, rq, jb), buf(DAY, rq, jb),
            buf(T, TR + 1, A, L), buf(T, TR + 1, A, L), buf(C * A, L), buf(XS, L),
            buf(DAY, I, S), buf(DAY, A, L), buf(T, 2, RP, B), buf(T, 2, RP, B),
            buf(DAY, 2, RP, B), buf(T, RP, B),
            dma(NB), dma(T), dma(T), dma(T), dma(T), dma(NB, DAY), dma(NB, DAY), dma(T), dma(T),
            dma(DAY), dma(DAY), dma(DAY), dma(DAY), dma(DAY), dma(DAY), dma(T), dma(T),
            dma(DAY), dma(DAY), dma(T), dma(T),
        ],
        compiler_params=pltpu.CompilerParams(
            collective_id=0, has_side_effects=True, vmem_limit_bytes=60 * 1024 * 1024
        ),
    )(
        coarse_var.astype(F32), fine_var.astype(F32), coarse.reshape(N, C * A, B), coarse_lat,
        coarse_lon, fine_lat, fine_lon, fine,
    )
    days = N * DAY
    small = o_small[0]
    return (
        o_flat,
        o_flon.reshape(R, jb).T,
        small[C * TR:C * TR + V * TR].reshape(V, TR) / math.sqrt(days * I * T * J),
        o_clat[:a_own, :S],
        o_fin[:, :rr].reshape(R, B).T,
        small[:C * TR].reshape(C, TR) / math.sqrt(days * S * R),
    )


def solution(mesh):
    in_specs = (
        P("day", None, "tile", None),
        P("day", None, "tile", None),
        P("tile", None),
        P(),
        P(),
        P("tile", None),
        P(),
        P(),
    )
    out_specs = (P("tile", None), P("tile", None), P(), P("tile", None), P(), P())
    return jax.shard_map(
        functools.partial(per_device, mesh.shape["tile"], mesh.shape["day"]),
        mesh=mesh, in_specs=in_specs, out_specs=out_specs, check_vma=False,
    )
```

```python
import functools
import math

import jax
import jax.numpy as jnp
from jax import lax
from jax.experimental import pallas as pl
from jax.experimental.pallas import tpu as pltpu
from jax.sharding import PartitionSpec as P

F32 = jnp.float32
BF16 = jnp.bfloat16
MESH = pl.DeviceIdType.MESH
LANES = 128


def dot(left, right):
    return jnp.dot(left, right, preferred_element_type=F32)


def dot_nt(left, right):
    return lax.dot_general(left, right, (((1,), (1,)), ((), ())), preferred_element_type=F32)


def halves(value):
    high = value.astype(BF16)
    return high, (value - high.astype(F32)).astype(BF16)


def dot_exact(left, right):
    high, low = halves(right)
    return dot(left, high) + dot(left, low)


def dot_nt_three(left, right):
    lh, ll = halves(left)
    rh, rl = halves(right)
    return dot_nt(lh, rh) + (dot_nt(lh, rl) + dot_nt(ll, rh))


def kernel(
    d,
    cvar, fvar, coarse, clat, clon, flat, flon, fine,
    o_flat, o_flon, o_fin, o_small, o_clat,
    fbuf, along, wall, wfl, core, mixed, lifted, lifted_t, lon_pad, lon_pad_t,
    back, spread, fva, gl, gday, gown, gtile, gfin,
    qsend, qpart, qrecv, vv, xs, lat_day, clat_day, fsend, frecv, fday, fall,
    s_fine, s_w, r_w, s_q, r_q, s_gd, r_gd, s_gt, r_gt, s_gf, r_gf,
    s_ld, r_ld, s_cd, r_cd, s_fs, r_fs, s_fd, r_fd, s_fa, r_fa, s_x, r_x, s_y, r_y,
):
    T, DAY, N, C, A, R, S, TR, V, I, J = (
        d["T"], d["DAY"], d["N"], d["C"], d["A"], d["R"], d["S"], d["TR"], d["V"], d["I"], d["J"]
    )
    JB, NB, NSUB, jb, rq, rr = d["JB"], d["NB"], d["NSUB"], d["jb"], d["rq"], d["rr"]
    L = N * R
    me = lax.axis_index("tile")
    day = lax.axis_index("day")
    first = lax.rem(lax.div(me * jb, JB) + 1, NB)

    def block_of(k):
        return lax.rem(first + k, NB)

    def fine_copy(k):
        columns = pl.ds(pl.multiple_of(block_of(k) * JB, JB), JB)
        return pltpu.make_async_copy(fine.at[:, :, :, columns], fbuf.at[k], s_fine.at[k])

    @pl.loop(0, NB)
    def _(k):
        fine_copy(k).start()

    barrier = pltpu.get_barrier_semaphore()

    @pl.loop(1, T)
    def _(off):
        pl.semaphore_signal(barrier, inc=1, device_id={"tile": lax.rem(me + off, T)}, device_id_type=MESH)

    @pl.loop(1, DAY)
    def _(off):
        pl.semaphore_signal(barrier, inc=1, device_id={"day": lax.rem(day + off, DAY)}, device_id_type=MESH)

    def tile_copy(src, dst, ssem, rsem, peer):
        return pltpu.make_async_remote_copy(
            src_ref=src, dst_ref=dst, send_sem=ssem, recv_sem=rsem,
            device_id={"tile": peer}, device_id_type=MESH,
        )

    def day_copy(src, dst, ssem, rsem, peer):
        return pltpu.make_async_remote_copy(
            src_ref=src, dst_ref=dst, send_sem=ssem, recv_sem=rsem,
            device_id={"day": peer}, device_id_type=MESH,
        )

    row = lax.broadcasted_iota(jnp.int32, (R, L), 0)
    column = lax.broadcasted_iota(jnp.int32, (R, L), 1)
    row_t = lax.broadcasted_iota(jnp.int32, (L, R), 0)
    column_t = lax.broadcasted_iota(jnp.int32, (L, R), 1)
    total = None
    for n in range(N):
        place_t = jnp.where(column_t + n * R == row_t, 1.0, 0.0).astype(BF16)
        factor_t = dot(place_t, clon[...]).astype(BF16)
        part = dot_nt(coarse[n], factor_t)
        total = part if total is None else total + part
    along[...] = total.reshape(C, A, L)
    for t in range(TR):
        acc = cvar[t, 0] * along[0]
        for c in range(1, C):
            acc = acc + cvar[t, c] * along[c]
        wall[me, t] = acc
    wall[me, TR] = jnp.zeros((A, L), F32)
    wall[me, TR, :, 0:S] = clat[...].astype(F32)

    pl.semaphore_wait(barrier, T - 1 + DAY - 1)

    H = T // 2
    pair, member = lax.div(me, 2), lax.rem(me, 2)
    partner = pair * 2 + 1 - member

    def ahead(off):
        return lax.rem(pair + off, H)

    def behind(off):
        return lax.rem(pair - off + H, H)

    def w_along(off):
        return tile_copy(wall.at[me], wall.at[me], s_w.at[off], r_w.at[off], ahead(off) * 2 + member)

    def w_along_in(off):
        slot = behind(off) * 2 + member
        return tile_copy(wall.at[slot], wall.at[slot], s_w.at[off], r_w.at[off], slot)

    def w_across(off):
        slot = behind(off) * 2 + member
        return tile_copy(wall.at[slot], wall.at[slot], s_x.at[off], r_x.at[off], partner)

    def w_across_in(off):
        slot = behind(off) * 2 + 1 - member
        return tile_copy(wall.at[slot], wall.at[slot], s_x.at[off], r_x.at[off], partner)

    @pl.loop(1, H)
    def _(off):
        w_along(off).start()

    w_across(0).start()

    for n in range(N):
        place = jnp.where(row + n * R == column, 1.0, 0.0).astype(BF16)
        place_t = jnp.where(column_t + n * R == row_t, 1.0, 0.0).astype(BF16)

        @pl.loop(0, NB)
        def _(b):
            rows = pl.ds(pl.multiple_of(b * JB, JB), JB)
            block_t = flon[:, rows]
            block = jnp.transpose(block_t.astype(F32)).astype(BF16)
            lon_pad[n, rows, :] = dot(block, place).astype(BF16)
            lon_pad_t[n, b] = dot(place_t, block_t).astype(BF16)

    back[...] = jnp.zeros_like(back)
    fva[...] = jnp.zeros_like(fva)
    xs[...] = jnp.zeros_like(xs)
    qsend[:, TR] = jnp.zeros((T, A, L), F32)
    if rr < 8:
        fsend[...] = jnp.zeros_like(fsend)

    @pl.loop(1, H)
    def _(off):
        w_along_in(off).wait_recv()
        w_across(off).start()

    @pl.loop(0, H)
    def _(off):
        w_across_in(off).wait_recv()

    for t in range(TR):
        wfl[:, t * L:(t + 1) * L] = wall[:, t].reshape(T * A, L)
    lat_all = wall[:, TR].reshape(T * A, L)
    lat_t = jnp.transpose(lat_all)[0:S].astype(BF16)
    core[...] = dot_exact(lat_t, wfl[...])
    mixed[...] = dot_exact(jnp.transpose(flat[...].astype(F32)).astype(BF16), core[...])

    CH = min(32, I)

    @pl.loop(0, I // CH)
    def _(q):
        rows = pl.ds(pl.multiple_of(q * CH, CH), CH)
        for v in range(V):
            acc = fvar[v, 0] * mixed[rows, 0:L]
            for t in range(1, TR):
                acc = acc + fvar[v, t] * mixed[rows, t * L:(t + 1) * L]
            lifted[v, rows, :] = acc.astype(BF16)

    for v in range(V):
        lifted_t[v] = jnp.transpose(lifted[v].astype(F32)).astype(BF16)

    def gd_send(k, off):
        to = lax.rem(day + off, DAY)
        return day_copy(
            gl.at[k, :, pl.ds(pl.multiple_of(to * rq, rq), rq), :], gday.at[k, day],
            s_gd.at[k, off], r_gd.at[k, off], to,
        )

    def gd_recv(k, off):
        source = lax.rem(day - off + DAY, DAY)
        return day_copy(
            gl.at[k, :, pl.ds(pl.multiple_of(day * rq, rq), rq), :], gday.at[k, source],
            s_gd.at[k, off], r_gd.at[k, off], source,
        )

    def gt_send(k, q, owner):
        off = lax.rem(owner - me + T, T)
        return tile_copy(gown.at[k, q], gtile.at[me], s_gt.at[off], r_gt.at[off], owner)

    def gt_recv(off):
        source = lax.rem(me - off + T, T)
        return tile_copy(gown.at[0, 0], gtile.at[source], s_gt.at[off], r_gt.at[off], source)

    def pass_on(k):
        for off in range(1, DAY):
            gd_recv(k, off).wait_recv()
        acc = gday[k, 0]
        for e in range(1, DAY):
            acc = acc + gday[k, e]
        gown[k] = acc
        for q in range(NSUB):
            owner = block_of(k) * NSUB + q

            @pl.when(owner != me)
            def _():
                gt_send(k, q, owner).start()

            @pl.when(owner == me)
            def _():
                gtile[me] = acc[q]

    @pl.loop(0, NB)
    def _(k):
        fine_copy(k).wait()
        b = block_of(k)
        rows = pl.ds(pl.multiple_of(b * JB, JB), JB)
        grad = None
        for v in range(V):
            term = None
            for n in range(N):
                predicted = dot(lifted[v], lon_pad_t[n, b])
                residual = (predicted - fbuf[k, n, v].astype(F32)).astype(BF16)
                part = dot(residual, lon_pad[n, rows, :])
                term = part if term is None else term + part
                piece = dot(lifted_t[v, n * R:(n + 1) * R, :], residual)
                grad = piece if grad is None else grad + piece
            back[v] += term
        for q in range(NSUB):
            gl[k, q] = grad[:, q * jb:(q + 1) * jb]
        gday[k, day] = gl[k, :, pl.ds(pl.multiple_of(day * rq, rq), rq), :]
        for off in range(1, DAY):
            gd_send(k, off).start()

        @pl.when(k >= 2)
        def _():
            pass_on(k - 2)

    @pl.loop(0, I // CH)
    def _(q):
        rows = pl.ds(pl.multiple_of(q * CH, CH), CH)
        for t in range(TR):
            acc = fvar[0, t] * back[0, rows, :]
            for v in range(1, V):
                acc = acc + fvar[v, t] * back[v, rows, :]
            spread[rows, t * L:(t + 1) * L] = acc

    scale = math.sqrt(S * R * TR / (I * T * J * V))
    core_grad = dot_exact(flat[...], spread[...]) * scale
    wanted = dot_exact(lat_all[:, 0:S].astype(BF16), core_grad)
    for t in range(TR):
        qsend[:, t] = wanted[:, t * L:(t + 1) * L].reshape(T, A, L)
    qsend[:, TR, :, 0:S] = dot_nt_three(wfl[...], core_grad).reshape(T, A, S)

    def q_across(off):
        slot = ahead(off) * 2 + 1 - member
        return tile_copy(qsend.at[slot], qpart.at[ahead(off)], s_y.at[off], r_y.at[off], partner)

    def q_send(off):
        return tile_copy(
            qpart.at[ahead(off)], qrecv.at[pair], s_q.at[off], r_q.at[off], ahead(off) * 2 + member
        )

    def q_recv(off):
        source = behind(off)
        return tile_copy(
            qpart.at[pair], qrecv.at[source], s_q.at[off], r_q.at[off], source * 2 + member
        )

    @pl.loop(1, H)
    def _(off):
        q_across(off).start()

    q_across(0).start()

    lat_day[day] = dot_nt_three(core[...], spread[...])

    @pl.loop(1, H)
    def _(off):
        q_across(off).wait_recv()
        slot = ahead(off)
        qpart[slot] = qpart[slot] + qsend[slot * 2 + member]
        q_send(off).start()

    q_across(0).wait_recv()
    qrecv[pair] = qpart[pair] + qsend[me]

    for k in range(max(NB - 2, 0), NB):
        pass_on(k)

    def own_send(buf, ssem, rsem, off):
        return day_copy(buf.at[day], buf.at[day], ssem.at[off], rsem.at[off], lax.rem(day + off, DAY))

    def own_recv(buf, ssem, rsem, off):
        source = lax.rem(day - off + DAY, DAY)
        return day_copy(buf.at[source], buf.at[source], ssem.at[off], rsem.at[off], source)

    for off in range(1, DAY):
        own_send(lat_day, s_ld, r_ld, off).start()

    @pl.loop(0, I // CH)
    def _(q):
        rows = pl.ds(pl.multiple_of(q * CH, CH), CH)
        for v in range(V):
            held = back[v, rows, :]
            for t in range(TR):
                product = held * mixed[rows, t * L:(t + 1) * L]
                fva[v * TR + t] += jnp.sum(product.reshape(CH // 8, 8, L), axis=0)

    xs[C * TR:C * TR + V * TR, :] = jnp.sum(fva[...], axis=1)

    @pl.loop(1, H)
    def _(off):
        q_recv(off).wait_recv()

    summed = qrecv[0]
    for p in range(1, H):
        summed = summed + qrecv[p]
    clat_day[day] = summed[TR]
    for off in range(1, DAY):
        own_send(clat_day, s_cd, r_cd, off).start()
    q_of = summed[0:TR]
    for c in range(C):
        acc = cvar[0, c] * q_of[0]
        for t in range(1, TR):
            acc = acc + cvar[t, c] * q_of[t]
        vv[c * A:(c + 1) * A, :] = acc
        xs[c * TR:(c + 1) * TR, :] = jnp.sum(along[c][None] * q_of, axis=1)
    v_high, v_low = halves(jnp.transpose(vv[...]))
    lon_t = None
    for n in range(N):
        mine = slice(n * R, (n + 1) * R)
        part = dot(v_high[mine], coarse[n]) + dot(v_low[mine], coarse[n])
        lon_t = part if lon_t is None else lon_t + part
    x_high, x_low = halves(xs[...])
    ones = jnp.ones((d["RP"], L), BF16)
    small = dot_nt(ones, x_high) + dot_nt(ones, x_low)
    B = lon_t.shape[1]
    for p in range(T):
        fsend[p, 0, 0:rr, :] = lon_t[p * rr:(p + 1) * rr, :]
        fsend[p, 1] = small
    frecv[me] = fsend[me]

    def f_send(off):
        peer = lax.rem(me + off, T)
        return tile_copy(fsend.at[peer], frecv.at[me], s_fs.at[off], r_fs.at[off], peer)

    def f_recv(off):
        source = lax.rem(me - off + T, T)
        return tile_copy(fsend.at[me], frecv.at[source], s_fs.at[off], r_fs.at[off], source)

    @pl.loop(1, T)
    def _(off):
        f_send(off).start()

    @pl.loop(1, T)
    def _(off):
        gt_recv(off).wait_recv()

    rows_sum = gtile[0]
    for p in range(1, T):
        rows_sum = rows_sum + gtile[p]
    gfin[day] = rows_sum
    for off in range(1, DAY):
        own_send(gfin, s_gf, r_gf, off).start()

    @pl.loop(1, T)
    def _(off):
        f_recv(off).wait_recv()

    fsum = frecv[0]
    for p in range(1, T):
        fsum = fsum + frecv[p]
    fday[day] = fsum
    for off in range(1, DAY):
        own_send(fday, s_fd, r_fd, off).start()

    for off in range(1, DAY):
        own_recv(lat_day, s_ld, r_ld, off).wait_recv()
    acc = lat_day[0]
    for e in range(1, DAY):
        acc = acc + lat_day[e]
    o_flat[...] = acc
    for off in range(1, DAY):
        own_recv(clat_day, s_cd, r_cd, off).wait_recv()
    acc = clat_day[0]
    for e in range(1, DAY):
        acc = acc + clat_day[e]
    o_clat[...] = acc

    for off in range(1, DAY):
        own_recv(fday, s_fd, r_fd, off).wait_recv()
    ftotal = fday[0]
    for e in range(1, DAY):
        ftotal = ftotal + fday[e]
    fall[me] = ftotal[0]

    def a_copy(slot, off, peer):
        return tile_copy(fall.at[slot], fall.at[slot], s_fa.at[off], r_fa.at[off], peer)

    @pl.loop(1, T)
    def _(off):
        a_copy(me, off, lax.rem(me + off, T)).start()

    o_small[...] = ftotal[1]
    for off in range(1, DAY):
        own_recv(gfin, s_gf, r_gf, off).wait_recv()
    o_flon[...] = gfin[...]

    @pl.loop(1, T)
    def _(off):
        a_copy(lax.rem(me - off + T, T), off, lax.rem(me + off, T)).wait_recv()

    o_fin[...] = fall[...]

    @pl.loop(1, T)
    def _(off):
        gt_recv(off).wait_send()
        f_send(off).wait_send()
        a_copy(me, off, lax.rem(me + off, T)).wait_send()

    @pl.loop(1, H)
    def _(off):
        w_along(off).wait_send()
        q_send(off).wait_send()

    @pl.loop(0, H)
    def _(off):
        w_across(off).wait_send()
        q_across(off).wait_send()

    for off in range(1, DAY):
        own_send(lat_day, s_ld, r_ld, off).wait_send()
        own_send(clat_day, s_cd, r_cd, off).wait_send()
        own_send(gfin, s_gf, r_gf, off).wait_send()
        own_send(fday, s_fd, r_fd, off).wait_send()

        @pl.loop(0, NB)
        def _(k):
            gd_send(k, off).wait_send()


def finish(d, days, flat, flon, fin, small, clat, o_flat, o_flon, o_fvar, o_clat, o_clon, o_cvar):
    T, DAY, C, R, S, TR, V, I, J = (
        d["T"], d["DAY"], d["C"], d["R"], d["S"], d["TR"], d["V"], d["I"], d["J"]
    )
    rq, rr = d["rq"], d["rr"]
    o_flat[...] = flat[...] * (1.0 / math.sqrt(days * V * J))
    for e in range(DAY):
        o_flon[e * rq:(e + 1) * rq, :] = flon[e] * (1.0 / math.sqrt(days * V * I * T))
    for p in range(T):
        o_clon[p * rr:(p + 1) * rr, :] = fin[p, 0:rr] * (1.0 / math.sqrt(days * S * TR))
    own = o_clat.shape[0]
    o_clat[...] = clat[0:own, 0:S] * (1.0 / math.sqrt(days * R * TR))
    width = small.shape[1]
    line = jnp.broadcast_to(small[0:1, :], (8, width))
    row = lax.broadcasted_iota(jnp.int32, (8, width), 0)
    lane = lax.broadcasted_iota(jnp.int32, (8, width), 1)
    at = lax.broadcasted_iota(jnp.int32, (LANES, width), 1)
    to = lax.broadcasted_iota(jnp.int32, (LANES, width), 0)

    def placed(kept, chosen):
        high, low = halves(jnp.where(kept, line, 0.0))
        chosen = jnp.where(chosen, 1.0, 0.0).astype(BF16)
        return dot_nt(high, chosen) + dot_nt(low, chosen)

    by_variable = placed(lax.rem(lane, TR) == row, lax.div(at, TR) == to)
    o_cvar[...] = by_variable[0:TR, 0:C] * (1.0 / math.sqrt(days * S * R))
    by_fine = placed(lax.div(lane, TR) == row + C, lax.rem(at, TR) == to)
    o_fvar[...] = by_fine[0:V, 0:TR] * (1.0 / math.sqrt(days * I * T * J))


def per_device(T, DAY, coarse, fine, coarse_lat, coarse_lon, coarse_var, fine_lat, fine_lon, fine_var):
    N, C, a_own, B = coarse.shape
    A = -(-a_own // 8) * 8
    if A != a_own:
        coarse = jnp.pad(coarse, ((0, 0), (0, 0), (0, A - a_own), (0, 0)))
        coarse_lat = jnp.pad(coarse_lat, ((0, A - a_own), (0, 0)))
    R, S, TR = coarse_lon.shape[1], coarse_lat.shape[1], coarse_var.shape[1]
    V, I, J = fine.shape[1], fine.shape[2], fine.shape[3]
    jb = J // T
    JB = max(512, jb)
    NB, NSUB = J // JB, JB // jb
    rq, rr = R // DAY, R // T
    RP = max(rr, 8)
    L = N * R
    W = TR * L
    XS = -(-(C * TR + V * TR) // LANES) * LANES
    XS = max(XS, B)
    d = dict(T=T, DAY=DAY, N=N, C=C, A=A, R=R, S=S, TR=TR, V=V, I=I, J=J,
             JB=JB, NB=NB, NSUB=NSUB, jb=jb, rq=rq, rr=rr, RP=RP)
    vmem = pl.BlockSpec(memory_space=pltpu.VMEM)
    smem = pl.BlockSpec(memory_space=pltpu.SMEM)
    dma = lambda *shape: pltpu.SemaphoreType.DMA(shape)
    buf = lambda *shape: pltpu.VMEM(shape, F32)
    half = lambda *shape: pltpu.VMEM(shape, BF16)
    o_flat, o_flon, o_fin, o_small, o_clat = pl.pallas_call(
        functools.partial(kernel, d),
        out_shape=(
            jax.ShapeDtypeStruct((S, I), F32),
            jax.ShapeDtypeStruct((DAY, rq, jb), F32),
            jax.ShapeDtypeStruct((T, RP, B), F32),
            jax.ShapeDtypeStruct((RP, XS), F32),
            jax.ShapeDtypeStruct((A, L), F32),
        ),
        in_specs=[smem, smem, vmem, vmem, vmem, vmem, vmem, pl.BlockSpec(memory_space=pl.ANY)],
        out_specs=(vmem,) * 5,
        scratch_shapes=[
            half(NB, N, V, I, JB), buf(C, A, L), buf(T, TR + 1, A, L), buf(T * A, W), buf(S, W),
            buf(I, W), half(V, I, L), half(V, L, I), half(N, J, L), half(N, NB, L, JB),
            buf(V, I, L), buf(I, W), buf(V * TR, 8, L), buf(NB, NSUB, R, jb),
            buf(NB, DAY, NSUB, rq, jb), buf(NB, NSUB, rq, jb), buf(T, rq, jb), buf(DAY, rq, jb),
            buf(T, TR + 1, A, L), buf(T // 2, TR + 1, A, L), buf(T // 2, TR + 1, A, L), buf(C * A, L), buf(XS, L),
            buf(DAY, S, I), buf(DAY, A, L), buf(T, 2, RP, B), buf(T, 2, RP, B),
            buf(DAY, 2, RP, B), buf(T, RP, B),
            dma(NB), dma(T), dma(T), dma(T), dma(T), dma(NB, DAY), dma(NB, DAY), dma(T), dma(T),
            dma(DAY), dma(DAY), dma(DAY), dma(DAY), dma(DAY), dma(DAY), dma(T), dma(T),
            dma(DAY), dma(DAY), dma(T), dma(T), dma(T), dma(T), dma(T), dma(T),
        ],
        compiler_params=pltpu.CompilerParams(
            collective_id=0, has_side_effects=True, vmem_limit_bytes=60 * 1024 * 1024
        ),
    )(
        coarse_var.T.astype(F32), fine_var.astype(F32), coarse.reshape(N, C * A, B), coarse_lat,
        coarse_lon.T, fine_lat.T, fine_lon.T, fine,
    )
    days = N * DAY
    flat_t, flon_t, fvar, clat, clon_t, cvar_t = pl.pallas_call(
        functools.partial(finish, d, days),
        out_shape=(
            jax.ShapeDtypeStruct((S, I), F32),
            jax.ShapeDtypeStruct((R, jb), F32),
            jax.ShapeDtypeStruct((V, TR), F32),
            jax.ShapeDtypeStruct((a_own, S), F32),
            jax.ShapeDtypeStruct((R, B), F32),
            jax.ShapeDtypeStruct((TR, C), F32),
        ),
        in_specs=[vmem] * 5,
        out_specs=(vmem,) * 6,
    )(o_flat, o_flon, o_fin, o_small, o_clat)
    return (flat_t.T, flon_t.T, fvar, clat, clon_t.T, cvar_t.T)


def solution(mesh):
    in_specs = (
        P("day", None, "tile", None),
        P("day", None, "tile", None),
        P("tile", None),
        P(),
        P(),
        P("tile", None),
        P(),
        P(),
    )
    out_specs = (P("tile", None), P("tile", None), P(), P("tile", None), P(), P())
    return jax.shard_map(
        functools.partial(per_device, mesh.shape["tile"], mesh.shape["day"]),
        mesh=mesh, in_specs=in_specs, out_specs=out_specs, check_vma=False,
    )
```
